32 devices in a mesh: row: 4 (over y, core), col: 8 (over z, x).
Axes of the slice: x: 2, y: 2, z: 4, core: 2. Of those that a mesh axis runs over, the one named last changes fastest.
Arguments:
- child_fronts: bfloat16 [128, 768, 768], P(('row', 'col')), as said below
- child_tiles: int32 [128, 2], P(('row', 'col')), may hold values from 0 to 7, as said below
- child_parent: int32 [128, 1], P(('row', 'col')), may hold values from 0 to 7; in each aligned block of 4 rows (0 to 3, 4 to 7, ...) at most 2 rows name the same one
- parent_front: float32 [8, 1024, 1024], P('col', 'row'), as said below
Outputs:
- child_lower: bfloat16 [128, 256, 512], P(('row', 'col'))
- parent_panel: float32 [8, 1024, 512], P('col', 'row')
- parent_rest: float32 [8, 1024, 512], P('col', 'row')
The draws below stay inside these ranges and needn't reach their ends.
Inputs may be any that keep to these rules, and one draw needn't show every extreme that they name: `child_tiles`: each child's block tiles are distinct and increasing. `child_parent`: among the children of one device no parent is named more than 2 times, a bound that some block reaches. `child_fronts`: each child front is symmetric positive definite. `parent_front`: each parent front is symmetric positive definite.
All inputs are finite; a program needn't handle non-finite values.
Results may differ from the reference program's by a relative error of at most 0.001.
Values sent between devices are 32-bit elements; how exact they have to be, the bound alone decides.
A program may use at most 128 MiB of HBM per device.

```python
import math
import jax
import jax.numpy as jnp
import numpy as np
from jax import lax

S1 = 512
TILE = 128
RT1 = 2
PT = 8
PT2 = 4
CAP = 2
KID_DEV = 4
R1 = 256
F1 = 768
F2 = 1024
S2 = 512
KIDS = 128
N_COL = 8


def node_kernel(points, scales):
    offset_x = points[:, None, 0] - points[None, :, 0]
    offset_y = points[:, None, 1] - points[None, :, 1]
    offset_z = points[:, None, 2] - points[None, :, 2]
    distance = jnp.sqrt(offset_x * offset_x + offset_y * offset_y + offset_z * offset_z)
    return scales[:, None] * scales[None, :] * jnp.exp(-2.0 * distance)


def node_scales(key_scale, key_ridge, count):
    scales = jax.random.uniform(key_scale, (count,), jnp.float32, 0.7, 1.4)
    ridge_values = jax.random.uniform(key_ridge, (count,), jnp.float32, 0.5, 1.5)
    return (scales, ridge_values)


def one_child(child_key):
    key_pivot, key_edge, key_scale, key_ridge = jax.random.split(child_key, 4)
    pivot_points = jax.random.uniform(key_pivot, (S1, 3), jnp.float32)
    edge_points = jax.random.uniform(key_edge, (R1, 3), jnp.float32)
    edge_points = edge_points * jnp.array([0.25, 1.0, 1.0], jnp.float32) + jnp.array([1.0, 0.0, 0.0], jnp.float32)
    points = jnp.concatenate([pivot_points, edge_points], axis=0)
    scales, ridge_values = node_scales(key_scale, key_ridge, F1)
    kernel_part = node_kernel(points, scales)
    is_pivot = jnp.arange(F1) < S1
    coupling = jnp.where(is_pivot[:, None] == is_pivot[None, :], jnp.float32(1.0), jnp.float32(0.6))
    result = 0.0625 * (kernel_part * coupling + ridge_values[:, None] * jnp.eye(F1, dtype=jnp.float32))
    return result.astype(jnp.bfloat16)


def draw_child_fronts(key, part):
    child_keys = jax.random.split(key, KIDS)
    return lax.map(one_child, child_keys)


def one_parent(parent_key):
    key_points, key_scale, key_ridge = jax.random.split(parent_key, 3)
    points = jax.random.uniform(key_points, (F2, 3), jnp.float32)
    scales, ridge_values = node_scales(key_scale, key_ridge, F2)
    kernel_part = node_kernel(points, scales)
    return 0.25 * kernel_part + 0.5 * ridge_values[:, None] * jnp.eye(F2, dtype=jnp.float32)


def draw_parent_front(key, part):
    parent_keys = jax.random.split(key, N_COL)
    return lax.map(one_parent, parent_keys)


def draw_child_tiles(key, part):
    base_rows = jnp.broadcast_to(jnp.arange(PT, dtype=jnp.int32), (KIDS, PT))
    shuffled = jax.random.permutation(key, base_rows, axis=1, independent=True)
    return jnp.sort(shuffled[:, :RT1], axis=1).astype(jnp.int32)


def routed_block(rng, own, number, rows, count, top, limit, skew):
    ranking = jax.random.permutation(rng, count)
    heavy_load, common = load_shares(count, rows * top, limit, skew, True), load_shares(count, rows * top, limit, skew, False)
    places = jnp.arange(count)

    def named(lengths, rotation):
        used = int((lengths > 0).sum())
        fixed = max(1, used // 4)
        shifted = fixed + (places - fixed + rotation * (used - fixed)) % max(1, count - fixed)
        return jnp.zeros((count,), jnp.int32).at[ranking[jnp.where(places < fixed, places, shifted)]].set(jnp.asarray(lengths, jnp.int32))

    lengths = jnp.where(number % 4 == 0, named(heavy_load, number // 4), named(common, number - number // 4 - 1))
    mixed = jax.random.permutation(jax.random.fold_in(own, 3), count)
    source_of, taker = mixed[0:count // 2 * 2:2], mixed[1:count // 2 * 2:2]
    margin = jnp.minimum(lengths[source_of] - 1, limit - lengths[taker]) // 2
    margin = jnp.where((source_of == ranking[0]) | (taker == ranking[0]) | (lengths[taker] == 0), 0, jnp.maximum(margin, 0))
    shifted = jax.random.randint(jax.random.fold_in(own, 4), (count // 2,), 0, 1 << 20) % (margin + 1)
    lengths = lengths.at[source_of].add(-shifted).at[taker].add(shifted)
    labels = jnp.searchsorted(jnp.cumsum(lengths), jnp.arange(rows * top), side="right").astype(jnp.int32)
    table = labels.reshape(top, rows).T
    table = table[jax.random.permutation(jax.random.fold_in(own, 1), rows)]
    rotation = jax.random.randint(jax.random.fold_in(own, 2), (rows, 1), 0, top)
    return jnp.take_along_axis(table, (jnp.arange(top)[None, :] + rotation) % top, axis=1)


def load_shares(amount, total, reach, slope, full):
    portions = [(1 << 20) // math.isqrt(grade ** slope) + 1 for grade in range(1, amount + 1)]
    largest = reach if full else min(reach, max(-(-total // amount), total * portions[0] // sum(portions)))
    least = 1 if total - largest >= amount - 1 else 0
    holding, rest = [largest] + [least] * (amount - 1), total - largest - least * (amount - 1)
    while rest > 0:
        free = [i for i in range(1, amount) if holding[i] < largest] or [i for i in range(1, amount) if holding[i] < reach]
        mass, left = sum([portions[i] for i in free]), rest
        for i in free:
            extra = min(reach - holding[i], max(1, left * portions[i] // mass), rest)
            holding[i] = holding[i] + extra
            rest = rest - extra
    return np.array(holding)


def setup_inputs(seed: int = 0) -> dict:
    key_list = jax.random.split(jax.random.key(seed), 5)
    child_fronts = draw_child_fronts(jax.random.fold_in(key_list[4], 71), 0)
    child_tiles = draw_child_tiles(jax.random.fold_in(key_list[4], 71), 0)
    child_parent_keys = jax.random.split(jax.random.fold_in(key_list[2], 1), KIDS // KID_DEV)
    child_parent_turns = jax.random.permutation(jax.random.fold_in(key_list[2], 3), KIDS // KID_DEV)
    child_parent = jax.vmap(lambda own, number: routed_block(jax.random.fold_in(key_list[2], 2), own, number, KID_DEV, N_COL, 1, CAP, 2))(child_parent_keys, child_parent_turns).reshape((KIDS, 1))
    parent_front = draw_parent_front(jax.random.fold_in(key_list[4], 71), 0)
    return dict(child_fronts=child_fronts, child_tiles=child_tiles, child_parent=child_parent, parent_front=parent_front)


def factor_child(front_block):
    whole_front = front_block.astype(jnp.float32)
    pivot_block = whole_front[:S1, :S1]
    below_block = whole_front[S1:, :S1]
    corner = whole_front[S1:, S1:]
    lower_factor = jnp.linalg.cholesky(pivot_block)
    child_panel = jax.scipy.linalg.solve_triangular(lower_factor, below_block.T, lower=True).T
    schur_block = corner - jnp.dot(child_panel, child_panel.T, precision=lax.Precision.HIGHEST)
    return (child_panel.astype(jnp.bfloat16), schur_block)

def factor_parent(front_rows):
    order_all = front_rows.shape[0]
    row_numbers = jnp.arange(order_all)
    columns_out = []
    for panel_index in range(PT2):
        start_col = panel_index * TILE
        diag_factor = jnp.linalg.cholesky(front_rows[start_col:start_col + TILE, start_col:start_col + TILE])
        column = jax.scipy.linalg.solve_triangular(diag_factor, front_rows[:, start_col:start_col + TILE].T, lower=True).T
        column = jnp.where((row_numbers >= start_col)[:, None], column, jnp.float32(0.0))
        front_rows = front_rows - jnp.dot(column, column.T, precision=lax.Precision.HIGHEST)
        columns_out.append(column)
    panel_all = jnp.concatenate(columns_out, axis=1)
    rest_all = jnp.where((row_numbers >= S2)[:, None], front_rows[:, S2:], jnp.float32(0.0))
    return (panel_all, rest_all)

def reference(child_fronts, child_tiles, child_parent, parent_front):
    child_lower, schurs = lax.map(factor_child, child_fronts)
    tile_blocks = schurs.reshape(KIDS, RT1, TILE, RT1, TILE).transpose(0, 1, 3, 2, 4)
    parent_ids = child_parent[:, 0]
    tile_grid = jnp.zeros((N_COL, PT, PT, TILE, TILE), jnp.float32)
    tile_grid = tile_grid.at[parent_ids[:, None, None], child_tiles[:, :, None], child_tiles[:, None, :]].add(tile_blocks)
    added = tile_grid.transpose(0, 1, 3, 2, 4).reshape(N_COL, F2, F2)
    parent_panel, parent_rest = lax.map(factor_parent, parent_front + added)
    return (child_lower, parent_panel, parent_rest)
```

```python
import functools
import jax
import jax.numpy as jnp
from jax import lax
from jax.experimental import pallas as pl
from jax.experimental.pallas import tpu as pltpu
from jax.sharding import PartitionSpec as P

S1 = 512
TILE = 128
RT1 = 2
PT = 8
PT2 = 4
CAP = 2
STRIP = 16
VMEM_BYTES = 56 * 1024 * 1024
F32 = jnp.float32


def split(x):
    hi = x.astype(jnp.bfloat16)
    lo = (x - hi.astype(F32)).astype(jnp.bfloat16)
    return hi, lo


def dot_nn(a, b):
    ah, al = split(a)
    bh, bl = split(b)
    return jnp.dot(
        jnp.concatenate([ah, ah, al], axis=1),
        jnp.concatenate([bh, bl, bh], axis=0),
        preferred_element_type=F32,
    )


def dot_tn(a, b):
    ah, al = split(a)
    bh, bl = split(b)
    return lax.dot_general(
        jnp.concatenate([ah, ah, al], axis=0),
        jnp.concatenate([bh, bl, bh], axis=0),
        (((0,), (0,)), ((), ())),
        preferred_element_type=F32,
    )


def factor_tiles(work, twin, kids):
    for first in range(0, TILE, STRIP):
        rows = [work[pl.ds(first + i, 2 * kids, stride=TILE), :] for i in range(STRIP)]
        heads = [twin[pl.ds(first + i, 2 * kids, stride=TILE), :] for i in range(STRIP)]
        coef = {}
        for i in range(STRIP):
            for k in range(i, STRIP):
                lane = heads[i][:, first + k : first + k + 1]
                coef[i, k] = jnp.broadcast_to(lane, (2 * kids, TILE))
        for j in range(STRIP):
            scale = lax.rsqrt(coef[j, j])
            line = {k: coef[j, k] * scale for k in range(j + 1, STRIP)}
            rows[j] = rows[j] * scale
            for i in range(j + 1, STRIP):
                for k in range(i, STRIP):
                    coef[i, k] = coef[i, k] - line[i] * line[k]
                rows[i] = rows[i] - line[i] * rows[j]
        for i in range(STRIP):
            work[pl.ds(first + i, 2 * kids, stride=TILE), :] = rows[i]
        after = first + STRIP
        if after == TILE:
            break
        for k in range(kids):
            upper = work[k * TILE + first : k * TILE + after, :]
            inverse = work[(kids + k) * TILE + first : (kids + k) * TILE + after, :]
            change = dot_tn(upper, jnp.concatenate([upper, inverse], axis=1))
            head = slice(k * TILE + after, (k + 1) * TILE)
            tail = slice((kids + k) * TILE + after, (kids + k + 1) * TILE)
            fresh = work[head, :] - change[after:, :TILE]
            work[head, :] = fresh
            twin[head, :] = fresh
            twin[tail, :] = fresh
            work[tail, :] = work[tail, :] - change[after:, TILE:]


def load_tile(work, twin, kids, k, tile):
    rows = pl.ds(k * TILE, TILE)
    mirror = pl.ds((kids + k) * TILE, TILE)
    work[rows, :] = tile
    twin[rows, :] = tile
    twin[mirror, :] = tile
    r = lax.broadcasted_iota(jnp.int32, (TILE, TILE), 0)
    c = lax.broadcasted_iota(jnp.int32, (TILE, TILE), 1)
    work[mirror, :] = jnp.where(r == c, 1.0, 0.0).astype(F32)


def child_kernel(target, fronts, lower, outgoing, front, work, twin):
    kids, order = fronts.shape[0], fronts.shape[1]
    tiles = order // TILE
    pivots = S1 // TILE

    def convert(k, _):
        for a in range(tiles):
            rows = slice(a * TILE, (a + 1) * TILE)
            front[k, rows, a * TILE :] = fronts[k, rows, a * TILE :].astype(F32)
        return 0

    lax.fori_loop(0, kids, convert, 0)

    def step(p, _):
        for q in range(pivots):

            @pl.when(p == q)
            def _():
                here = slice(q * TILE, (q + 1) * TILE)
                for k in range(kids):
                    load_tile(work, twin, kids, k, front[k, here, here])

        factor_tiles(work, twin, kids)
        for q in range(pivots):

            @pl.when(p == q)
            def _():
                here = slice(q * TILE, (q + 1) * TILE)
                edge = (q + 1) * TILE

                def apply(k, _):
                    inverse = work[pl.ds((kids + k) * TILE, TILE), :]
                    x = dot_nn(inverse, front[k, here, edge:])
                    xt = x.T
                    lower[k, :, here] = xt[S1 - edge :, :].astype(jnp.bfloat16)
                    th, tl = split(xt)
                    xh, xl = split(x)
                    left = jnp.concatenate([th, th, tl], axis=1)
                    right = jnp.concatenate([xh, xl, xh], axis=0)
                    for a in range(q + 1, tiles):
                        rows = slice(a * TILE, (a + 1) * TILE)
                        off = (a - q - 1) * TILE
                        fresh = front[k, rows, a * TILE :] - jnp.dot(
                            left[off : off + TILE, :], right[:, off:], preferred_element_type=F32
                        )
                        if q < pivots - 1:
                            front[k, rows, a * TILE :] = fresh
                        elif a == pivots:
                            outgoing[target[k], :TILE, :] = fresh[:, :TILE]
                            outgoing[target[k], TILE : 2 * TILE, :] = fresh[:, TILE:]
                        else:
                            outgoing[target[k], 2 * TILE :, :] = fresh
                    return 0

                lax.fori_loop(0, kids, apply, 0)

        return 0

    lax.fori_loop(0, pivots, step, 0)


def tile_number(a, b):
    return a * PT - a * (a - 1) // 2 + (b - a)


def gather_kernel(tiles, slots, parent, dense):
    dense[...] = jnp.zeros_like(dense)
    band = parent.shape[0] // TILE
    first = lax.axis_index("row") * band
    for n in range(band):
        for b in range(PT):

            @pl.when(b >= first + n)
            def _():
                dense[tile_number(first + n, b)] = parent[
                    n * TILE : (n + 1) * TILE, b * TILE : (b + 1) * TILE
                ]

    def add(s, _):
        t0 = tiles[s, 0]
        t1 = tiles[s, 1]

        @pl.when(t1 > 0)
        def _():
            for m, (a, b) in enumerate(((t0, t0), (t0, t1), (t1, t1))):
                n = tile_number(a, b)
                dense[n] = dense[n] + slots[s, m * TILE : (m + 1) * TILE, :]

        return 0

    lax.fori_loop(0, slots.shape[0], add, 0)


def parent_kernel(dense, panel, rest, front, column, work, twin):
    height = panel.shape[0]
    split_row = PT2 * TILE
    for a in range(PT):
        for b in range(a, PT):
            tile = dense[tile_number(a, b)]
            front[a * TILE : (a + 1) * TILE, b * TILE : (b + 1) * TILE] = tile
            if PT2 <= a < b:
                front[b * TILE : (b + 1) * TILE, a * TILE : (a + 1) * TILE] = tile.T
    column[...] = jnp.zeros_like(column)
    r = lax.broadcasted_iota(jnp.int32, (TILE, TILE), 0)
    c = lax.broadcasted_iota(jnp.int32, (TILE, TILE), 1)

    def step(p, _):
        for q in range(PT2):

            @pl.when(p == q)
            def _():
                here = slice(q * TILE, (q + 1) * TILE)
                load_tile(work, twin, 1, 0, front[here, here])

        factor_tiles(work, twin, 1)
        for q in range(PT2):

            @pl.when(p == q)
            def _():
                here = slice(q * TILE, (q + 1) * TILE)
                edge = (q + 1) * TILE
                column[here, here] = jnp.where(r >= c, work[:TILE, :].T, 0.0)
                x = dot_nn(work[TILE:, :], front[here, edge:])
                xt = x.T
                column[edge:, here] = xt
                th, tl = split(xt)
                xh, xl = split(x)
                left = jnp.concatenate([th, th, tl], axis=1)
                right = jnp.concatenate([xh, xl, xh], axis=0)
                for a in range(q + 1, PT):
                    rows = slice(a * TILE, (a + 1) * TILE)
                    start = min(a, PT2) * TILE
                    off = a * TILE - edge
                    front[rows, start:] = front[rows, start:] - jnp.dot(
                        left[off : off + TILE, :],
                        right[:, start - edge :],
                        preferred_element_type=F32,
                    )

        return 0

    lax.fori_loop(0, PT2, step, 0)
    first = pl.multiple_of(lax.axis_index("row") * height, TILE)
    panel[...] = column[pl.ds(first, height), :]

    @pl.when(first >= split_row)
    def _():
        rest[...] = front[pl.ds(first, height), split_row:]

    @pl.when(first < split_row)
    def _():
        rest[...] = jnp.zeros_like(rest)


def params():
    return pltpu.CompilerParams(vmem_limit_bytes=VMEM_BYTES)


VM = pl.BlockSpec(memory_space=pltpu.VMEM)
SM = pl.BlockSpec(memory_space=pltpu.SMEM)


def run_children(fronts, target, slots):
    kids, order, _ = fronts.shape
    return pl.pallas_call(
        child_kernel,
        in_specs=[SM, VM],
        out_specs=[VM, VM],
        out_shape=[
            jax.ShapeDtypeStruct((kids, order - S1, S1), jnp.bfloat16),
            jax.ShapeDtypeStruct((slots, 3 * TILE, TILE), F32),
        ],
        scratch_shapes=[
            pltpu.VMEM((kids, order, order), F32),
            pltpu.VMEM((2 * kids * TILE, TILE), F32),
            pltpu.VMEM((2 * kids * TILE, TILE), F32),
        ],
        compiler_params=params(),
        name="children",
    )(target, fronts)


def run_gather(tiles, slots, parent):
    return pl.pallas_call(
        gather_kernel,
        in_specs=[SM, VM, VM],
        out_specs=VM,
        out_shape=jax.ShapeDtypeStruct((PT * (PT + 1) // 2, TILE, TILE), F32),
        compiler_params=params(),
        name="assemble",
    )(tiles, slots, parent)


def run_parent(dense, height):
    return pl.pallas_call(
        parent_kernel,
        in_specs=[VM],
        out_specs=[VM, VM],
        out_shape=[
            jax.ShapeDtypeStruct((height, PT2 * TILE), F32),
            jax.ShapeDtypeStruct((height, (PT - PT2) * TILE), F32),
        ],
        scratch_shapes=[
            pltpu.VMEM((PT * TILE, PT * TILE), F32),
            pltpu.VMEM((PT * TILE, PT2 * TILE), F32),
            pltpu.VMEM((2 * TILE, TILE), F32),
            pltpu.VMEM((2 * TILE, TILE), F32),
        ],
        compiler_params=params(),
        name="parent",
    )(dense)


def local(child_fronts, child_tiles, child_parent, parent_front):
    groups = lax.axis_size("col")
    kid_count = child_parent.shape[0]
    parent_ids = child_parent[:, 0]
    kid_order = jnp.arange(kid_count)
    earlier = (parent_ids[:, None] == parent_ids[None, :]) & (
        kid_order[None, :] < kid_order[:, None]
    )
    slot_index = jnp.sum(earlier.astype(jnp.int32), axis=1)
    target = parent_ids * CAP + slot_index
    chosen = target[None, :] == jnp.arange(groups * CAP)[:, None]
    outgoing_tiles = jnp.sum(
        jnp.where(chosen[:, :, None], child_tiles[None, :, :], 0), axis=1
    ).astype(jnp.int32)
    child_lower, outgoing = run_children(child_fronts, target, groups * CAP)
    received = lax.all_to_all(outgoing, "col", split_axis=0, concat_axis=0, tiled=True)
    received_tiles = lax.all_to_all(
        outgoing_tiles, "col", split_axis=0, concat_axis=0, tiled=True
    )
    dense = run_gather(received_tiles, received, parent_front[0])
    dense = lax.psum(dense, "row")
    parent_panel, parent_rest = run_parent(dense, parent_front.shape[1])
    return (child_lower, parent_panel[None], parent_rest[None])


def solution(mesh):
    placed = (
        P(("row", "col"), None, None),
        P(("row", "col"), None),
        P(("row", "col"), None),
        P("col", "row", None),
    )
    return jax.shard_map(
        local,
        mesh=mesh,
        in_specs=placed,
        out_specs=(P(("row", "col"), None, None), P("col", "row", None), P("col", "row", None)),
        check_vma=False,
    )
```

```python
import functools
import jax
import jax.numpy as jnp
from jax import lax
from jax.experimental import pallas as pl
from jax.experimental.pallas import tpu as pltpu
from jax.sharding import PartitionSpec as P

S1 = 512
TILE = 128
RT1 = 2
PT = 8
PT2 = 4
CAP = 2
STRIP = 16
EXTRA = 8
PIVOT_TILES = PT2 * (PT2 + 1) // 2
ALL_TILES = PT * (PT + 1) // 2
VMEM_BYTES = 56 * 1024 * 1024
F32 = jnp.float32


def split(x):
    hi = x.astype(jnp.bfloat16)
    lo = (x - hi.astype(F32)).astype(jnp.bfloat16)
    return hi, lo


def dot_nn(a, b):
    ah, al = split(a)
    bh, bl = split(b)
    return jnp.dot(
        jnp.concatenate([ah, ah, al], axis=1),
        jnp.concatenate([bh, bl, bh], axis=0),
        preferred_element_type=F32,
    )


def dot_tn(a, b):
    ah, al = split(a)
    bh, bl = split(b)
    return lax.dot_general(
        jnp.concatenate([ah, ah, al], axis=0),
        jnp.concatenate([bh, bl, bh], axis=0),
        (((0,), (0,)), ((), ())),
        preferred_element_type=F32,
    )


def factor_tiles(work, twin, kids):
    for first in range(0, TILE, STRIP):
        rows = [work[pl.ds(first + i, 2 * kids, stride=TILE), :] for i in range(STRIP)]
        heads = [twin[pl.ds(first + i, 2 * kids, stride=TILE), :] for i in range(STRIP)]
        coef = {}
        for i in range(STRIP):
            for k in range(i, STRIP):
                lane = heads[i][:, first + k : first + k + 1]
                coef[i, k] = jnp.broadcast_to(lane, (2 * kids, TILE))
        for j in range(STRIP):
            scale = lax.rsqrt(coef[j, j])
            line = {k: coef[j, k] * scale for k in range(j + 1, STRIP)}
            rows[j] = rows[j] * scale
            for i in range(j + 1, STRIP):
                for k in range(i, STRIP):
                    coef[i, k] = coef[i, k] - line[i] * line[k]
                rows[i] = rows[i] - line[i] * rows[j]
        for i in range(STRIP):
            work[pl.ds(first + i, 2 * kids, stride=TILE), :] = rows[i]
        after = first + STRIP
        if after == TILE:
            break
        for k in range(kids):
            upper = work[k * TILE + first : k * TILE + after, :]
            inverse = work[(kids + k) * TILE + first : (kids + k) * TILE + after, :]
            change = dot_tn(upper, jnp.concatenate([upper, inverse], axis=1))
            head = slice(k * TILE + after, (k + 1) * TILE)
            tail = slice((kids + k) * TILE + after, (kids + k + 1) * TILE)
            fresh = work[head, :] - change[after:, :TILE]
            work[head, :] = fresh
            twin[head, :] = fresh
            twin[tail, :] = fresh
            work[tail, :] = work[tail, :] - change[after:, TILE:]


def load_tile(work, twin, kids, k, tile):
    rows = pl.ds(k * TILE, TILE)
    mirror = pl.ds((kids + k) * TILE, TILE)
    work[rows, :] = tile
    twin[rows, :] = tile
    twin[mirror, :] = tile
    r = lax.broadcasted_iota(jnp.int32, (TILE, TILE), 0)
    c = lax.broadcasted_iota(jnp.int32, (TILE, TILE), 1)
    work[mirror, :] = jnp.where(r == c, 1.0, 0.0).astype(F32)


def child_kernel(parents, places, fronts, lower, outgoing, front, work, twin):
    kids, order = fronts.shape[0], fronts.shape[1]
    tiles = order // TILE
    pivots = S1 // TILE
    row = lax.broadcasted_iota(jnp.int32, (TILE, TILE), 0)
    lane = lax.broadcasted_iota(jnp.int32, (TILE, TILE), 1)
    outgoing[:, 2 * TILE :, :] = jnp.zeros((outgoing.shape[0], EXTRA, TILE), F32)

    def convert(k, _):
        for a in range(tiles):
            rows = slice(a * TILE, (a + 1) * TILE)
            front[k, rows, a * TILE :] = fronts[k, rows, a * TILE :].astype(F32)
        return 0

    lax.fori_loop(0, kids, convert, 0)

    def send(k, top, corner):
        slot = parents[k, 0] * CAP
        for other in range(kids):
            same = (parents[other, 0] == parents[k, 0]) & (other < k)
            slot = slot + same.astype(jnp.int32)
        outgoing[slot, :TILE, :] = top[:, TILE:]
        outgoing[slot, TILE : 2 * TILE, :] = jnp.where(row <= lane, top[:, :TILE], corner)
        diagonal = jnp.sum(jnp.where(row == lane, corner, 0.0), axis=0, keepdims=True)
        r = row[:EXTRA]
        c = lane[:EXTRA]
        ids = jnp.where(c == 0, places[k, 0], places[k, 1]).astype(F32)
        outgoing[slot, 2 * TILE :, :] = jnp.where(
            r == 0, jnp.broadcast_to(diagonal, (EXTRA, TILE)), ids
        )

    def step(p, _):
        for q in range(pivots):

            @pl.when(p == q)
            def _():
                here = slice(q * TILE, (q + 1) * TILE)
                for k in range(kids):
                    load_tile(work, twin, kids, k, front[k, here, here])

        factor_tiles(work, twin, kids)
        for q in range(pivots):

            @pl.when(p == q)
            def _():
                here = slice(q * TILE, (q + 1) * TILE)
                edge = (q + 1) * TILE

                def apply(k, _):
                    inverse = work[pl.ds((kids + k) * TILE, TILE), :]
                    x = dot_nn(inverse, front[k, here, edge:])
                    xt = x.T
                    lower[k, :, here] = xt[S1 - edge :, :].astype(jnp.bfloat16)
                    th, tl = split(xt)
                    xh, xl = split(x)
                    left = jnp.concatenate([th, th, tl], axis=1)
                    right = jnp.concatenate([xh, xl, xh], axis=0)
                    last = []
                    for a in range(q + 1, tiles):
                        rows = slice(a * TILE, (a + 1) * TILE)
                        off = (a - q - 1) * TILE
                        fresh = front[k, rows, a * TILE :] - jnp.dot(
                            left[off : off + TILE, :], right[:, off:], preferred_element_type=F32
                        )
                        if q < pivots - 1:
                            front[k, rows, a * TILE :] = fresh
                        else:
                            last.append(fresh)
                    if last:
                        send(k, *last)
                    return 0

                lax.fori_loop(0, kids, apply, 0)

        return 0

    lax.fori_loop(0, pivots, step, 0)


def corner_number(a, b):
    return a * PT2 - a * (a - 1) // 2 + (b - a)


def tile_number(a, b):
    if isinstance(a, int) and isinstance(b, int):
        if b < PT2:
            return corner_number(a, b)
        if a < PT2:
            return PIVOT_TILES + a * PT2 + b - PT2
        return PIVOT_TILES + PT2 * PT2 + corner_number(a - PT2, b - PT2)
    beside = PIVOT_TILES + a * PT2 + b - PT2
    after = PIVOT_TILES + PT2 * PT2 + corner_number(a - PT2, b - PT2)
    return jnp.where(b < PT2, corner_number(a, b), jnp.where(a < PT2, beside, after))


def gather_kernel(tiles, slots, parent, dense):
    dense[...] = jnp.zeros_like(dense)
    band = parent.shape[0] // TILE
    first = lax.axis_index("row") * band
    row = lax.broadcasted_iota(jnp.int32, (TILE, TILE), 0)
    lane = lax.broadcasted_iota(jnp.int32, (TILE, TILE), 1)
    for n in range(band):
        for b in range(PT):

            @pl.when(b >= first + n)
            def _():
                dense[tile_number(first + n, b)] = parent[
                    n * TILE : (n + 1) * TILE, b * TILE : (b + 1) * TILE
                ]

    def add(s, _):
        t0 = tiles[s, 0]
        t1 = tiles[s, 1]

        @pl.when(t1 > 0)
        def _():
            both = slots[s, TILE : 2 * TILE, :]
            diagonal = jnp.broadcast_to(slots[s, 2 * TILE : 2 * TILE + 1, :], (TILE, TILE))
            n = tile_number(t0, t0)
            dense[n] = dense[n] + jnp.where(row <= lane, both, 0.0)
            n = tile_number(t0, t1)
            dense[n] = dense[n] + slots[s, :TILE, :]
            n = tile_number(t1, t1)
            mirrored = jnp.where(row < lane, both.T, 0.0)
            dense[n] = dense[n] + jnp.where(row == lane, diagonal, mirrored)

        return 0

    lax.fori_loop(0, slots.shape[0], add, 0)


def parent_kernel(
    ranks, dense, panel, rest, front, column, work, twin, inverses, total, fetched, halves, heard,
    core_send, core_recv, far_send, far_recv, back_send, back_recv,
):
    height = panel.shape[0]
    cut = PT2 * TILE
    me = lax.axis_index("row")
    core = lax.rem(me, 2)
    place = lax.div(me, 2)
    chips = ranks // 2
    partner = place * 2 + 1 - core
    peers = [lax.rem(place + d, chips) * 2 + core for d in range(1, chips)]
    other_half = PT2 * PT2 + PIVOT_TILES
    parts = ((0, PIVOT_TILES // 2, 0), (PIVOT_TILES, other_half // 2, PIVOT_TILES // 2))

    barrier = pltpu.get_barrier_semaphore()
    for device in [partner] + peers:
        pl.semaphore_signal(
            barrier, inc=1, device_id={"row": device}, device_id_type=pl.DeviceIdType.MESH
        )
    pl.semaphore_wait(barrier, chips)

    def copy(source, target, send, recv, device):
        return pltpu.make_async_remote_copy(
            src_ref=source,
            dst_ref=target,
            send_sem=send,
            recv_sem=recv,
            device_id={"row": device},
            device_id_type=pl.DeviceIdType.MESH,
        )

    near, far, back = [], [], []
    for i, (base, n, off) in enumerate(parts):
        near.append(
            copy(
                dense.at[pl.ds(base + (1 - core) * n, n)],
                fetched.at[pl.ds(off, n)],
                core_send.at[i],
                core_recv.at[i],
                partner,
            )
        )
        near[i].start()
    for i, (base, n, off) in enumerate(parts):
        near[i].wait()
        here = pl.ds(off, n)
        halves[here] = dense[pl.ds(base + core * n, n)] + fetched[here]
        far.append(
            [
                copy(halves.at[here], heard.at[d, here], far_send.at[i, d], far_recv.at[i, d], peer)
                for d, peer in enumerate(peers)
            ]
        )
        for one in far[i]:
            one.start()

    def finish(i):
        base, n, off = parts[i]
        mine = pl.ds(base + core * n, n)
        here = pl.ds(off, n)
        for one in far[i]:
            one.wait()
        value = halves[here]
        for d in range(len(peers)):
            value = value + heard[d, here]
        total[mine] = value
        back = copy(total.at[mine], total.at[mine], back_send.at[i], back_recv.at[i], partner)
        back.start()
        back.wait()

    finish(0)
    for a in range(PT2):
        for b in range(a, PT2):
            front[a * TILE : (a + 1) * TILE, b * TILE : (b + 1) * TILE] = total[tile_number(a, b)]
    column[...] = jnp.zeros_like(column)
    r = lax.broadcasted_iota(jnp.int32, (TILE, TILE), 0)
    c = lax.broadcasted_iota(jnp.int32, (TILE, TILE), 1)

    def step(p, _):
        for q in range(PT2):

            @pl.when(p == q)
            def _():
                here = slice(q * TILE, (q + 1) * TILE)
                load_tile(work, twin, 1, 0, front[here, here])

        factor_tiles(work, twin, 1)
        for q in range(PT2):

            @pl.when(p == q)
            def _():
                here = slice(q * TILE, (q + 1) * TILE)
                edge = (q + 1) * TILE
                column[here, here] = jnp.where(r >= c, work[:TILE, :].T, 0.0)
                inverses[q] = work[TILE:, :]
                if q == PT2 - 1:
                    return
                x = dot_nn(work[TILE:, :], front[here, edge:cut])
                xt = x.T
                column[edge:cut, here] = xt
                front[edge:cut, edge:cut] = front[edge:cut, edge:cut] - dot_nn(xt, x)

        return 0

    lax.fori_loop(0, PT2, step, 0)
    finish(1)
    for q in range(PT2):
        here = slice(q * TILE, (q + 1) * TILE)
        right = jnp.concatenate([total[tile_number(q, b)] for b in range(PT2, PT)], axis=1)
        if q:
            right = right - dot_nn(column[here, : q * TILE], front[: q * TILE, cut:])
        front[here, cut:] = dot_nn(inverses[q], right)
    x = front[:cut, cut:]
    xt = x.T
    column[cut:, :] = xt
    for a in range(PT2, PT):
        for b in range(a, PT):
            tile = total[tile_number(a, b)]
            if a == b:
                tile = jnp.where(r <= c, tile, tile.T)
            else:
                front[b * TILE : (b + 1) * TILE, a * TILE : (a + 1) * TILE] = tile.T
            front[a * TILE : (a + 1) * TILE, b * TILE : (b + 1) * TILE] = tile
    front[cut:, cut:] = front[cut:, cut:] - dot_nn(xt, x)
    first = pl.multiple_of(me * height, TILE)
    panel[...] = column[pl.ds(first, height), :]

    @pl.when(first >= cut)
    def _():
        rest[...] = front[pl.ds(first, height), cut:]

    @pl.when(first < cut)
    def _():
        rest[...] = jnp.zeros_like(rest)


def params(**more):
    return pltpu.CompilerParams(vmem_limit_bytes=VMEM_BYTES, **more)


VM = pl.BlockSpec(memory_space=pltpu.VMEM)
SM = pl.BlockSpec(memory_space=pltpu.SMEM)


def run_children(fronts, parents, places, slots):
    kids, order, _ = fronts.shape
    return pl.pallas_call(
        child_kernel,
        in_specs=[SM, SM, VM],
        out_specs=[VM, VM],
        out_shape=[
            jax.ShapeDtypeStruct((kids, order - S1, S1), jnp.bfloat16),
            jax.ShapeDtypeStruct((slots, 2 * TILE + EXTRA, TILE), F32),
        ],
        scratch_shapes=[
            pltpu.VMEM((kids, order, order), F32),
            pltpu.VMEM((2 * kids * TILE, TILE), F32),
            pltpu.VMEM((2 * kids * TILE, TILE), F32),
        ],
        compiler_params=params(),
        name="children",
    )(parents, places, fronts)


def run_gather(tiles, slots, parent):
    return pl.pallas_call(
        gather_kernel,
        in_specs=[SM, VM, VM],
        out_specs=VM,
        out_shape=jax.ShapeDtypeStruct((ALL_TILES, TILE, TILE), F32),
        compiler_params=params(),
        name="assemble",
    )(tiles, slots, parent)


def run_parent(dense, height):
    ranks = lax.axis_size("row")
    peers = max(1, ranks // 2 - 1)
    half = ALL_TILES // 2
    dma = pltpu.SemaphoreType.DMA
    return pl.pallas_call(
        functools.partial(parent_kernel, ranks),
        in_specs=[VM],
        out_specs=[VM, VM],
        out_shape=[
            jax.ShapeDtypeStruct((height, PT2 * TILE), F32),
            jax.ShapeDtypeStruct((height, (PT - PT2) * TILE), F32),
        ],
        scratch_shapes=[
            pltpu.VMEM((PT * TILE, PT * TILE), F32),
            pltpu.VMEM((PT * TILE, PT2 * TILE), F32),
            pltpu.VMEM((2 * TILE, TILE), F32),
            pltpu.VMEM((2 * TILE, TILE), F32),
            pltpu.VMEM((PT2, TILE, TILE), F32),
            pltpu.VMEM((ALL_TILES, TILE, TILE), F32),
            pltpu.VMEM((half, TILE, TILE), F32),
            pltpu.VMEM((half, TILE, TILE), F32),
            pltpu.VMEM((peers, half, TILE, TILE), F32),
            dma((2,)),
            dma((2,)),
            dma((2, peers)),
            dma((2, peers)),
            dma((2,)),
            dma((2,)),
        ],
        compiler_params=params(collective_id=1, has_side_effects=True),
        name="parent",
    )(dense)


def local(child_fronts, child_tiles, child_parent, parent_front):
    groups = lax.axis_size("col")
    child_lower, outgoing = run_children(child_fronts, child_parent, child_tiles, groups * CAP)
    received = lax.all_to_all(outgoing, "col", split_axis=0, concat_axis=0, tiled=True)
    received_tiles = received[:, 2 * TILE + 1, :RT1].astype(jnp.int32)
    dense = run_gather(received_tiles, received, parent_front[0])
    parent_panel, parent_rest = run_parent(dense, parent_front.shape[1])
    return (child_lower, parent_panel[None], parent_rest[None])


def solution(mesh):
    placed = (
        P(("row", "col"), None, None),
        P(("row", "col"), None),
        P(("row", "col"), None),
        P("col", "row", None),
    )
    return jax.shard_map(
        local,
        mesh=mesh,
        in_specs=placed,
        out_specs=(P(("row", "col"), None, None), P("col", "row", None), P("col", "row", None)),
        check_vma=False,
    )
```

```python
import functools
import jax
import jax.numpy as jnp
from jax import lax
from jax.experimental import pallas as pl
from jax.experimental.pallas import tpu as pltpu
from jax.sharding import PartitionSpec as P

S1 = 512
TILE = 128
RT1 = 2
PT = 8
PT2 = 4
CAP = 2
STRIP = 16
EXTRA = 8
SLOT = 2 * TILE + EXTRA
CHUNKS = 3
PIVOT_TILES = PT2 * (PT2 + 1) // 2
ALL_TILES = PT * (PT + 1) // 2
VMEM_BYTES = 56 * 1024 * 1024
F32 = jnp.float32


def split(x):
    hi = x.astype(jnp.bfloat16)
    lo = (x - hi.astype(F32)).astype(jnp.bfloat16)
    return hi, lo


def dot_nn(a, b):
    ah, al = split(a)
    bh, bl = split(b)
    return jnp.dot(
        jnp.concatenate([ah, ah, al], axis=1),
        jnp.concatenate([bh, bl, bh], axis=0),
        preferred_element_type=F32,
    )


def dot_tn(a, b):
    ah, al = split(a)
    bh, bl = split(b)
    return lax.dot_general(
        jnp.concatenate([ah, ah, al], axis=0),
        jnp.concatenate([bh, bl, bh], axis=0),
        (((0,), (0,)), ((), ())),
        preferred_element_type=F32,
    )


def factor_tiles(work, twin, kids):
    for first in range(0, TILE, STRIP):
        rows = [work[pl.ds(first + i, 2 * kids, stride=TILE), :] for i in range(STRIP)]
        heads = [twin[pl.ds(first + i, 2 * kids, stride=TILE), :] for i in range(STRIP)]
        coef = {}
        for i in range(STRIP):
            for k in range(i, STRIP):
                lane = heads[i][:, first + k : first + k + 1]
                coef[i, k] = jnp.broadcast_to(lane, (2 * kids, TILE))
        for j in range(STRIP):
            scale = lax.rsqrt(coef[j, j])
            line = {k: coef[j, k] * scale for k in range(j + 1, STRIP)}
            rows[j] = rows[j] * scale
            for i in range(j + 1, STRIP):
                for k in range(i, STRIP):
                    coef[i, k] = coef[i, k] - line[i] * line[k]
                rows[i] = rows[i] - line[i] * rows[j]
        for i in range(STRIP):
            work[pl.ds(first + i, 2 * kids, stride=TILE), :] = rows[i]
        after = first + STRIP
        if after == TILE:
            break
        for k in range(kids):
            upper = work[k * TILE + first : k * TILE + after, :]
            inverse = work[(kids + k) * TILE + first : (kids + k) * TILE + after, :]
            change = dot_tn(upper, jnp.concatenate([upper, inverse], axis=1))
            head = slice(k * TILE + after, (k + 1) * TILE)
            tail = slice((kids + k) * TILE + after, (kids + k + 1) * TILE)
            fresh = work[head, :] - change[after:, :TILE]
            work[head, :] = fresh
            twin[head, :] = fresh
            twin[tail, :] = fresh
            work[tail, :] = work[tail, :] - change[after:, TILE:]


def load_tile(work, twin, kids, k, tile):
    rows = pl.ds(k * TILE, TILE)
    mirror = pl.ds((kids + k) * TILE, TILE)
    work[rows, :] = tile
    twin[rows, :] = tile
    twin[mirror, :] = tile
    r = lax.broadcasted_iota(jnp.int32, (TILE, TILE), 0)
    c = lax.broadcasted_iota(jnp.int32, (TILE, TILE), 1)
    work[mirror, :] = jnp.where(r == c, 1.0, 0.0).astype(F32)


def child_kernel(groups, parents, places, fronts, lower, near, far, front, work, twin):
    kids, order = fronts.shape[0], fronts.shape[1]
    tiles = order // TILE
    pivots = S1 // TILE
    row = lax.broadcasted_iota(jnp.int32, (TILE, TILE), 0)
    lane = lax.broadcasted_iota(jnp.int32, (TILE, TILE), 1)
    near[:, :EXTRA, :] = jnp.zeros((near.shape[0], EXTRA, TILE), F32)
    half = groups // 2
    base = lax.div(lax.axis_index("col"), half) * half

    def convert(k, _):
        for a in range(tiles):
            rows = slice(a * TILE, (a + 1) * TILE)
            front[k, rows, a * TILE :] = fronts[k, rows, a * TILE :].astype(F32)
        return 0

    lax.fori_loop(0, kids, convert, 0)

    def send(k, top, corner):
        slot = parents[k, 0] * CAP
        for other in range(kids):
            same = (parents[other, 0] == parents[k, 0]) & (other < k)
            slot = slot + same.astype(jnp.int32)
        slot = slot - base * CAP
        inside = (slot >= 0) & (slot < half * CAP)
        crossed = jnp.where(slot < 0, slot + half * CAP, slot - half * CAP)
        code = jnp.where(inside, -1, crossed)
        diagonal = jnp.sum(jnp.where(row == lane, corner, 0.0), axis=0, keepdims=True)
        r = row[:EXTRA]
        c = lane[:EXTRA]
        ids = jnp.where(c == 0, places[k, 0], jnp.where(c == 1, places[k, 1], code)).astype(F32)
        far[k, :EXTRA, :] = jnp.where(r == 0, jnp.broadcast_to(diagonal, (EXTRA, TILE)), ids)
        far[k, EXTRA : EXTRA + TILE, :] = top[:, TILE:]
        far[k, EXTRA + TILE :, :] = jnp.where(row <= lane, top[:, :TILE], corner)

        @pl.when(inside)
        def _():
            near[slot] = far[k]

    def step(p, _):
        for q in range(pivots):

            @pl.when(p == q)
            def _():
                here = slice(q * TILE, (q + 1) * TILE)
                for k in range(kids):
                    load_tile(work, twin, kids, k, front[k, here, here])

        factor_tiles(work, twin, kids)
        for q in range(pivots):

            @pl.when(p == q)
            def _():
                here = slice(q * TILE, (q + 1) * TILE)
                edge = (q + 1) * TILE

                def apply(k, _):
                    inverse = work[pl.ds((kids + k) * TILE, TILE), :]
                    x = dot_nn(inverse, front[k, here, edge:])
                    xt = x.T
                    lower[k, :, here] = xt[S1 - edge :, :].astype(jnp.bfloat16)
                    th, tl = split(xt)
                    xh, xl = split(x)
                    left = jnp.concatenate([th, th, tl], axis=1)
                    right = jnp.concatenate([xh, xl, xh], axis=0)
                    last = []
                    for a in range(q + 1, tiles):
                        rows = slice(a * TILE, (a + 1) * TILE)
                        off = (a - q - 1) * TILE
                        fresh = front[k, rows, a * TILE :] - jnp.dot(
                            left[off : off + TILE, :], right[:, off:], preferred_element_type=F32
                        )
                        if q < pivots - 1:
                            front[k, rows, a * TILE :] = fresh
                        else:
                            last.append(fresh)
                    if last:
                        send(k, *last)
                    return 0

                lax.fori_loop(0, kids, apply, 0)

        return 0

    lax.fori_loop(0, pivots, step, 0)


def corner_number(a, b):
    return a * PT2 - a * (a - 1) // 2 + (b - a)


def tile_number(a, b):
    if isinstance(a, int) and isinstance(b, int):
        if b < PT2:
            return corner_number(a, b)
        if a < PT2:
            return PIVOT_TILES + a * PT2 + b - PT2
        return PIVOT_TILES + PT2 * PT2 + corner_number(a - PT2, b - PT2)
    beside = PIVOT_TILES + a * PT2 + b - PT2
    after = PIVOT_TILES + PT2 * PT2 + corner_number(a - PT2, b - PT2)
    return jnp.where(b < PT2, corner_number(a, b), jnp.where(a < PT2, beside, after))


def gather_kernel(tiles, slots, parent, dense):
    dense[...] = jnp.zeros_like(dense)
    band = parent.shape[0] // TILE
    first = lax.axis_index("row") * band
    row = lax.broadcasted_iota(jnp.int32, (TILE, TILE), 0)
    lane = lax.broadcasted_iota(jnp.int32, (TILE, TILE), 1)
    for n in range(band):
        for b in range(PT):

            @pl.when(b >= first + n)
            def _():
                dense[tile_number(first + n, b)] = parent[
                    n * TILE : (n + 1) * TILE, b * TILE : (b + 1) * TILE
                ]

    def add(s, _):
        t0 = tiles[s, 0]
        t1 = tiles[s, 1]

        @pl.when(t1 > 0)
        def _():
            both = slots[s, EXTRA + TILE :, :]
            diagonal = jnp.broadcast_to(slots[s, 0:1, :], (TILE, TILE))
            n = tile_number(t0, t0)
            dense[n] = dense[n] + jnp.where(row <= lane, both, 0.0)
            n = tile_number(t0, t1)
            dense[n] = dense[n] + slots[s, EXTRA : EXTRA + TILE, :]
            n = tile_number(t1, t1)
            mirrored = jnp.where(row < lane, both.T, 0.0)
            dense[n] = dense[n] + jnp.where(row == lane, diagonal, mirrored)

        return 0

    lax.fori_loop(0, slots.shape[0], add, 0)


def exchange_kernel(
    groups, near, far, received, arrived, relayed, far_send, far_recv, near_send, near_recv,
    relay_send, relay_recv,
):
    half = groups // 2
    kids = far.shape[0]
    me = lax.axis_index("col")
    spot = lax.rem(me, half)
    base = me - spot
    across = lax.rem(me + half, groups)
    mates = [lax.rem(spot + d, half) for d in range(1, half)]
    size = SLOT // CHUNKS
    chunks = [pl.ds(n * size, size) for n in range(CHUNKS)]

    barrier = pltpu.get_barrier_semaphore()
    for device in [across] + [base + mate for mate in mates]:
        pl.semaphore_signal(
            barrier, inc=1, device_id={"col": device}, device_id_type=pl.DeviceIdType.MESH
        )
    pl.semaphore_wait(barrier, half)

    def copy(source, target, send, recv, device):
        one = pltpu.make_async_remote_copy(
            src_ref=source,
            dst_ref=target,
            send_sem=send,
            recv_sem=recv,
            device_id={"col": device},
            device_id_type=pl.DeviceIdType.MESH,
        )
        one.start()
        return one

    crossing = [
        copy(far.at[:, rows], arrived.at[:, rows], far_send.at[n], far_recv.at[n], across)
        for n, rows in enumerate(chunks)
    ]
    pending = [
        copy(
            near.at[pl.ds(mate * CAP, CAP)],
            received.at[pl.ds((d + 1) * CAP, CAP)],
            near_send.at[d],
            near_recv.at[d],
            base + mate,
        )
        for d, mate in enumerate(mates)
    ]
    received[:CAP] = near[pl.ds(spot * CAP, CAP)]
    codes = None
    for n, rows in enumerate(chunks):
        crossing[n].wait()
        if codes is None:
            codes = [
                jnp.broadcast_to(arrived[k, 1:2, 2:3], (size, TILE)) for k in range(kids)
            ]

        def sort(slot, _):
            value = jnp.zeros((size, TILE), F32)
            for k in range(kids):
                value = jnp.where(codes[k] == slot.astype(F32), arrived[k, rows, :], value)
            relayed[slot, rows, :] = value
            return 0

        lax.fori_loop(0, half * CAP, sort, 0)
        for d, mate in enumerate(mates):
            pending.append(
                copy(
                    relayed.at[pl.ds(mate * CAP, CAP), rows],
                    received.at[pl.ds((half + d + 1) * CAP, CAP), rows],
                    relay_send.at[n, d],
                    relay_recv.at[n, d],
                    base + mate,
                )
            )
        received[half * CAP : (half + 1) * CAP, rows, :] = relayed[pl.ds(spot * CAP, CAP), rows, :]
    for one in pending:
        one.wait()


def parent_kernel(
    ranks, dense, panel, rest, front, column, work, twin, inverses, total, fetched, halves, heard,
    core_send, core_recv, far_send, far_recv, back_send, back_recv,
):
    height = panel.shape[0]
    cut = PT2 * TILE
    me = lax.axis_index("row")
    core = lax.rem(me, 2)
    place = lax.div(me, 2)
    chips = ranks // 2
    partner = place * 2 + 1 - core
    peers = [lax.rem(place + d, chips) * 2 + core for d in range(1, chips)]
    other_half = PT2 * PT2 + PIVOT_TILES
    parts = ((0, PIVOT_TILES // 2, 0), (PIVOT_TILES, other_half // 2, PIVOT_TILES // 2))

    barrier = pltpu.get_barrier_semaphore()
    for device in [partner] + peers:
        pl.semaphore_signal(
            barrier, inc=1, device_id={"row": device}, device_id_type=pl.DeviceIdType.MESH
        )
    pl.semaphore_wait(barrier, chips)

    def copy(source, target, send, recv, device):
        return pltpu.make_async_remote_copy(
            src_ref=source,
            dst_ref=target,
            send_sem=send,
            recv_sem=recv,
            device_id={"row": device},
            device_id_type=pl.DeviceIdType.MESH,
        )

    near, far, back = [], [], []
    for i, (base, n, off) in enumerate(parts):
        near.append(
            copy(
                dense.at[pl.ds(base + (1 - core) * n, n)],
                fetched.at[pl.ds(off, n)],
                core_send.at[i],
                core_recv.at[i],
                partner,
            )
        )
        near[i].start()
    for i, (base, n, off) in enumerate(parts):
        near[i].wait()
        here = pl.ds(off, n)
        halves[here] = dense[pl.ds(base + core * n, n)] + fetched[here]
        far.append(
            [
                copy(halves.at[here], heard.at[d, here], far_send.at[i, d], far_recv.at[i, d], peer)
                for d, peer in enumerate(peers)
            ]
        )
        for one in far[i]:
            one.start()

    def finish(i):
        base, n, off = parts[i]
        mine = pl.ds(base + core * n, n)
        here = pl.ds(off, n)
        for one in far[i]:
            one.wait()
        value = halves[here]
        for d in range(len(peers)):
            value = value + heard[d, here]
        total[mine] = value
        back = copy(total.at[mine], total.at[mine], back_send.at[i], back_recv.at[i], partner)
        back.start()
        back.wait()

    finish(0)
    for a in range(PT2):
        for b in range(a, PT2):
            front[a * TILE : (a + 1) * TILE, b * TILE : (b + 1) * TILE] = total[tile_number(a, b)]
    column[...] = jnp.zeros_like(column)
    r = lax.broadcasted_iota(jnp.int32, (TILE, TILE), 0)
    c = lax.broadcasted_iota(jnp.int32, (TILE, TILE), 1)

    def step(p, _):
        for q in range(PT2):

            @pl.when(p == q)
            def _():
                here = slice(q * TILE, (q + 1) * TILE)
                load_tile(work, twin, 1, 0, front[here, here])

        factor_tiles(work, twin, 1)
        for q in range(PT2):

            @pl.when(p == q)
            def _():
                here = slice(q * TILE, (q + 1) * TILE)
                edge = (q + 1) * TILE
                column[here, here] = jnp.where(r >= c, work[:TILE, :].T, 0.0)
                inverses[q] = work[TILE:, :]
                if q == PT2 - 1:
                    return
                x = dot_nn(work[TILE:, :], front[here, edge:cut])
                xt = x.T
                column[edge:cut, here] = xt
                front[edge:cut, edge:cut] = front[edge:cut, edge:cut] - dot_nn(xt, x)

        return 0

    lax.fori_loop(0, PT2, step, 0)
    finish(1)
    for q in range(PT2):
        here = slice(q * TILE, (q + 1) * TILE)
        right = jnp.concatenate([total[tile_number(q, b)] for b in range(PT2, PT)], axis=1)
        if q:
            right = right - dot_nn(column[here, : q * TILE], front[: q * TILE, cut:])
        front[here, cut:] = dot_nn(inverses[q], right)
    x = front[:cut, cut:]
    xt = x.T
    column[cut:, :] = xt
    for a in range(PT2, PT):
        for b in range(a, PT):
            tile = total[tile_number(a, b)]
            if a == b:
                tile = jnp.where(r <= c, tile, tile.T)
            else:
                front[b * TILE : (b + 1) * TILE, a * TILE : (a + 1) * TILE] = tile.T
            front[a * TILE : (a + 1) * TILE, b * TILE : (b + 1) * TILE] = tile
    front[cut:, cut:] = front[cut:, cut:] - dot_nn(xt, x)
    first = pl.multiple_of(me * height, TILE)
    panel[...] = column[pl.ds(first, height), :]

    @pl.when(first >= cut)
    def _():
        rest[...] = front[pl.ds(first, height), cut:]

    @pl.when(first < cut)
    def _():
        rest[...] = jnp.zeros_like(rest)


def params(**more):
    return pltpu.CompilerParams(vmem_limit_bytes=VMEM_BYTES, **more)


VM = pl.BlockSpec(memory_space=pltpu.VMEM)
SM = pl.BlockSpec(memory_space=pltpu.SMEM)


def run_children(fronts, parents, places, groups):
    kids, order, _ = fronts.shape
    return pl.pallas_call(
        functools.partial(child_kernel, groups),
        in_specs=[SM, SM, VM],
        out_specs=[VM, VM, VM],
        out_shape=[
            jax.ShapeDtypeStruct((kids, order - S1, S1), jnp.bfloat16),
            jax.ShapeDtypeStruct((groups // 2 * CAP, SLOT, TILE), F32),
            jax.ShapeDtypeStruct((kids, SLOT, TILE), F32),
        ],
        scratch_shapes=[
            pltpu.VMEM((kids, order, order), F32),
            pltpu.VMEM((2 * kids * TILE, TILE), F32),
            pltpu.VMEM((2 * kids * TILE, TILE), F32),
        ],
        compiler_params=params(),
        name="children",
    )(parents, places, fronts)


def run_exchange(near, far, groups):
    mates = groups // 2 - 1
    dma = pltpu.SemaphoreType.DMA
    return pl.pallas_call(
        functools.partial(exchange_kernel, groups),
        in_specs=[VM, VM],
        out_specs=VM,
        out_shape=jax.ShapeDtypeStruct((groups * CAP, SLOT, TILE), F32),
        scratch_shapes=[
            pltpu.VMEM(far.shape, F32),
            pltpu.VMEM(near.shape, F32),
            dma((CHUNKS,)),
            dma((CHUNKS,)),
            dma((mates,)),
            dma((mates,)),
            dma((CHUNKS, mates)),
            dma((CHUNKS, mates)),
        ],
        compiler_params=params(collective_id=2, has_side_effects=True),
        name="exchange",
    )(near, far)


def run_gather(tiles, slots, parent):
    return pl.pallas_call(
        gather_kernel,
        in_specs=[SM, VM, VM],
        out_specs=VM,
        out_shape=jax.ShapeDtypeStruct((ALL_TILES, TILE, TILE), F32),
        compiler_params=params(),
        name="assemble",
    )(tiles, slots, parent)


def run_parent(dense, height):
    ranks = lax.axis_size("row")
    peers = max(1, ranks // 2 - 1)
    half = ALL_TILES // 2
    dma = pltpu.SemaphoreType.DMA
    return pl.pallas_call(
        functools.partial(parent_kernel, ranks),
        in_specs=[VM],
        out_specs=[VM, VM],
        out_shape=[
            jax.ShapeDtypeStruct((height, PT2 * TILE), F32),
            jax.ShapeDtypeStruct((height, (PT - PT2) * TILE), F32),
        ],
        scratch_shapes=[
            pltpu.VMEM((PT * TILE, PT * TILE), F32),
            pltpu.VMEM((PT * TILE, PT2 * TILE), F32),
            pltpu.VMEM((2 * TILE, TILE), F32),
            pltpu.VMEM((2 * TILE, TILE), F32),
            pltpu.VMEM((PT2, TILE, TILE), F32),
            pltpu.VMEM((ALL_TILES, TILE, TILE), F32),
            pltpu.VMEM((half, TILE, TILE), F32),
            pltpu.VMEM((half, TILE, TILE), F32),
            pltpu.VMEM((peers, half, TILE, TILE), F32),
            dma((2,)),
            dma((2,)),
            dma((2, peers)),
            dma((2, peers)),
            dma((2,)),
            dma((2,)),
        ],
        compiler_params=params(collective_id=1, has_side_effects=True),
        name="parent",
    )(dense)


def local(child_fronts, child_tiles, child_parent, parent_front):
    groups = lax.axis_size("col")
    child_lower, near, far = run_children(child_fronts, child_parent, child_tiles, groups)
    received = run_exchange(near, far, groups)
    received_tiles = received[:, 1, :RT1].astype(jnp.int32)
    dense = run_gather(received_tiles, received, parent_front[0])
    parent_panel, parent_rest = run_parent(dense, parent_front.shape[1])
    return (child_lower, parent_panel[None], parent_rest[None])


def solution(mesh):
    placed = (
        P(("row", "col"), None, None),
        P(("row", "col"), None),
        P(("row", "col"), None),
        P("col", "row", None),
    )
    return jax.shard_map(
        local,
        mesh=mesh,
        in_specs=placed,
        out_specs=(P(("row", "col"), None, None), P("col", "row", None), P("col", "row", None)),
        check_vma=False,
    )
```

```python
import functools
import jax
import jax.numpy as jnp
from jax import lax
from jax.experimental import pallas as pl
from jax.experimental.pallas import tpu as pltpu
from jax.sharding import PartitionSpec as P

S1 = 512
TILE = 128
RT1 = 2
PT = 8
PT2 = 4
CAP = 2
STRIP = 16
EXTRA = 8
SLOT = 2 * TILE + EXTRA
CHUNKS = 3
PIVOT_TILES = PT2 * (PT2 + 1) // 2
ALL_TILES = PT * (PT + 1) // 2
VMEM_BYTES = 56 * 1024 * 1024
F32 = jnp.float32


def split(x):
    hi = x.astype(jnp.bfloat16)
    lo = (x - hi.astype(F32)).astype(jnp.bfloat16)
    return hi, lo


def dot_nn(a, b):
    ah, al = split(a)
    bh, bl = split(b)
    return jnp.dot(
        jnp.concatenate([ah, ah, al], axis=1),
        jnp.concatenate([bh, bl, bh], axis=0),
        preferred_element_type=F32,
    )


def dot_tn(a, b):
    ah, al = split(a)
    bh, bl = split(b)
    return lax.dot_general(
        jnp.concatenate([ah, ah, al], axis=0),
        jnp.concatenate([bh, bl, bh], axis=0),
        (((0,), (0,)), ((), ())),
        preferred_element_type=F32,
    )


def factor_tiles(work, twin, kids):
    for first in range(0, TILE, STRIP):
        rows = [work[pl.ds(first + i, 2 * kids, stride=TILE), :] for i in range(STRIP)]
        heads = [twin[pl.ds(first + i, 2 * kids, stride=TILE), :] for i in range(STRIP)]
        coef = {}
        for i in range(STRIP):
            for k in range(i, STRIP):
                lane = heads[i][:, first + k : first + k + 1]
                coef[i, k] = jnp.broadcast_to(lane, (2 * kids, TILE))
        for j in range(STRIP):
            scale = lax.rsqrt(coef[j, j])
            line = {k: coef[j, k] * scale for k in range(j + 1, STRIP)}
            rows[j] = rows[j] * scale
            for i in range(j + 1, STRIP):
                for k in range(i, STRIP):
                    coef[i, k] = coef[i, k] - line[i] * line[k]
                rows[i] = rows[i] - line[i] * rows[j]
        for i in range(STRIP):
            work[pl.ds(first + i, 2 * kids, stride=TILE), :] = rows[i]
        after = first + STRIP
        if after == TILE:
            break
        for k in range(kids):
            upper = work[k * TILE + first : k * TILE + after, :]
            inverse = work[(kids + k) * TILE + first : (kids + k) * TILE + after, :]
            change = dot_tn(upper, jnp.concatenate([upper, inverse], axis=1))
            head = slice(k * TILE + after, (k + 1) * TILE)
            tail = slice((kids + k) * TILE + after, (kids + k + 1) * TILE)
            fresh = work[head, :] - change[after:, :TILE]
            work[head, :] = fresh
            twin[head, :] = fresh
            twin[tail, :] = fresh
            work[tail, :] = work[tail, :] - change[after:, TILE:]


def load_tile(work, twin, kids, k, tile):
    rows = pl.ds(k * TILE, TILE)
    mirror = pl.ds((kids + k) * TILE, TILE)
    work[rows, :] = tile
    twin[rows, :] = tile
    twin[mirror, :] = tile
    r = lax.broadcasted_iota(jnp.int32, (TILE, TILE), 0)
    c = lax.broadcasted_iota(jnp.int32, (TILE, TILE), 1)
    work[mirror, :] = jnp.where(r == c, 1.0, 0.0).astype(F32)


def child_kernel(
    groups, parents_far, places_far, fronts, lower, near, far, front, work, twin, parents, places, loads
):
    fetches = [
        pltpu.make_async_copy(parents_far, parents, loads.at[0]),
        pltpu.make_async_copy(places_far, places, loads.at[1]),
    ]
    for one in fetches:
        one.start()
    kids, order = fronts.shape[0], fronts.shape[1]
    tiles = order // TILE
    pivots = S1 // TILE
    row = lax.broadcasted_iota(jnp.int32, (TILE, TILE), 0)
    lane = lax.broadcasted_iota(jnp.int32, (TILE, TILE), 1)
    near[:, :EXTRA, :] = jnp.zeros((near.shape[0], EXTRA, TILE), F32)
    half = groups // 2
    base = lax.div(lax.axis_index("col"), half) * half

    def read(q, k, rows, lanes):
        if q == 0:
            return fronts[k, rows, lanes].astype(F32)
        return front[k, rows, lanes]

    def send(k, top, corner):
        slot = parents[k, 0] * CAP
        for other in range(kids):
            same = (parents[other, 0] == parents[k, 0]) & (other < k)
            slot = slot + same.astype(jnp.int32)
        slot = slot - base * CAP
        inside = (slot >= 0) & (slot < half * CAP)
        crossed = jnp.where(slot < 0, slot + half * CAP, slot - half * CAP)
        code = jnp.where(inside, -1, crossed)
        diagonal = jnp.sum(jnp.where(row == lane, corner, 0.0), axis=0, keepdims=True)
        r = row[:EXTRA]
        c = lane[:EXTRA]
        ids = jnp.where(c == 0, places[k, 0], jnp.where(c == 1, places[k, 1], code)).astype(F32)
        far[k, :EXTRA, :] = jnp.where(r == 0, jnp.broadcast_to(diagonal, (EXTRA, TILE)), ids)
        far[k, EXTRA : EXTRA + TILE, :] = top[:, TILE:]
        far[k, EXTRA + TILE :, :] = jnp.where(row <= lane, top[:, :TILE], corner)

        @pl.when(inside)
        def _():
            near[slot] = far[k]

    def step(p, _):
        for q in range(pivots):

            @pl.when(p == q)
            def _():
                here = slice(q * TILE, (q + 1) * TILE)
                for k in range(kids):
                    load_tile(work, twin, kids, k, read(q, k, here, here))

        factor_tiles(work, twin, kids)
        for q in range(pivots):

            @pl.when(p == q)
            def _():
                here = slice(q * TILE, (q + 1) * TILE)
                edge = (q + 1) * TILE

                if q == pivots - 1:
                    for one in fetches:
                        one.wait()

                def apply(k, _):
                    inverse = work[pl.ds((kids + k) * TILE, TILE), :]
                    x = dot_nn(inverse, read(q, k, here, slice(edge, order)))
                    xt = x.T
                    lower[k, :, here] = xt[S1 - edge :, :].astype(jnp.bfloat16)
                    th, tl = split(xt)
                    xh, xl = split(x)
                    left = jnp.concatenate([th, th, tl], axis=1)
                    right = jnp.concatenate([xh, xl, xh], axis=0)
                    last = []
                    for a in range(q + 1, tiles):
                        rows = slice(a * TILE, (a + 1) * TILE)
                        off = (a - q - 1) * TILE
                        fresh = read(q, k, rows, slice(a * TILE, order)) - jnp.dot(
                            left[off : off + TILE, :], right[:, off:], preferred_element_type=F32
                        )
                        if q < pivots - 1:
                            front[k, rows, a * TILE :] = fresh
                        else:
                            last.append(fresh)
                    if last:
                        send(k, *last)
                    return 0

                lax.fori_loop(0, kids, apply, 0)

        return 0

    lax.fori_loop(0, pivots, step, 0)


def corner_number(a, b):
    return a * PT2 - a * (a - 1) // 2 + (b - a)


def tile_number(a, b):
    if isinstance(a, int) and isinstance(b, int):
        if b < PT2:
            return corner_number(a, b)
        if a < PT2:
            return PIVOT_TILES + a * PT2 + b - PT2
        return PIVOT_TILES + PT2 * PT2 + corner_number(a - PT2, b - PT2)
    beside = PIVOT_TILES + a * PT2 + b - PT2
    after = PIVOT_TILES + PT2 * PT2 + corner_number(a - PT2, b - PT2)
    return jnp.where(b < PT2, corner_number(a, b), jnp.where(a < PT2, beside, after))


def gather_kernel(tiles, slots, parent, dense):
    dense[...] = jnp.zeros_like(dense)
    band = parent.shape[0] // TILE
    first = lax.axis_index("row") * band
    row = lax.broadcasted_iota(jnp.int32, (TILE, TILE), 0)
    lane = lax.broadcasted_iota(jnp.int32, (TILE, TILE), 1)
    for n in range(band):
        for b in range(PT):

            @pl.when(b >= first + n)
            def _():
                dense[tile_number(first + n, b)] = parent[
                    n * TILE : (n + 1) * TILE, b * TILE : (b + 1) * TILE
                ]

    def add(s, _):
        t0 = tiles[s, 0]
        t1 = tiles[s, 1]

        @pl.when(t1 > 0)
        def _():
            both = slots[s, EXTRA + TILE :, :]
            diagonal = jnp.broadcast_to(slots[s, 0:1, :], (TILE, TILE))
            n = tile_number(t0, t0)
            dense[n] = dense[n] + jnp.where(row <= lane, both, 0.0)
            n = tile_number(t0, t1)
            dense[n] = dense[n] + slots[s, EXTRA : EXTRA + TILE, :]
            n = tile_number(t1, t1)
            mirrored = jnp.where(row < lane, both.T, 0.0)
            dense[n] = dense[n] + jnp.where(row == lane, diagonal, mirrored)

        return 0

    lax.fori_loop(0, slots.shape[0], add, 0)


def exchange_kernel(
    groups, near, far, received, arrived, relayed, far_send, far_recv, near_send, near_recv,
    relay_send, relay_recv,
):
    half = groups // 2
    kids = far.shape[0]
    me = lax.axis_index("col")
    spot = lax.rem(me, half)
    base = me - spot
    across = lax.rem(me + half, groups)
    mates = [lax.rem(spot + d, half) for d in range(1, half)]
    size = SLOT // CHUNKS
    chunks = [pl.ds(n * size, size) for n in range(CHUNKS)]

    barrier = pltpu.get_barrier_semaphore()
    for device in [across] + [base + mate for mate in mates]:
        pl.semaphore_signal(
            barrier, inc=1, device_id={"col": device}, device_id_type=pl.DeviceIdType.MESH
        )
    pl.semaphore_wait(barrier, half)

    def copy(source, target, send, recv, device):
        one = pltpu.make_async_remote_copy(
            src_ref=source,
            dst_ref=target,
            send_sem=send,
            recv_sem=recv,
            device_id={"col": device},
            device_id_type=pl.DeviceIdType.MESH,
        )
        one.start()
        return one

    crossing = [
        copy(far.at[:, rows], arrived.at[:, rows], far_send.at[n], far_recv.at[n], across)
        for n, rows in enumerate(chunks)
    ]
    pending = [
        copy(
            near.at[pl.ds(mate * CAP, CAP)],
            received.at[pl.ds((d + 1) * CAP, CAP)],
            near_send.at[d],
            near_recv.at[d],
            base + mate,
        )
        for d, mate in enumerate(mates)
    ]
    received[:CAP] = near[pl.ds(spot * CAP, CAP)]
    codes = None
    for n, rows in enumerate(chunks):
        crossing[n].wait()
        if codes is None:
            codes = [
                jnp.broadcast_to(arrived[k, 1:2, 2:3], (size, TILE)) for k in range(kids)
            ]

        def sort(slot, _):
            value = jnp.zeros((size, TILE), F32)
            for k in range(kids):
                value = jnp.where(codes[k] == slot.astype(F32), arrived[k, rows, :], value)
            relayed[slot, rows, :] = value
            return 0

        lax.fori_loop(0, half * CAP, sort, 0)
        for d, mate in enumerate(mates):
            pending.append(
                copy(
                    relayed.at[pl.ds(mate * CAP, CAP), rows],
                    received.at[pl.ds((half + d + 1) * CAP, CAP), rows],
                    relay_send.at[n, d],
                    relay_recv.at[n, d],
                    base + mate,
                )
            )
        received[half * CAP : (half + 1) * CAP, rows, :] = relayed[pl.ds(spot * CAP, CAP), rows, :]
    for one in pending:
        one.wait()


def parent_kernel(
    ranks, dense, panel, rest, front, column, work, twin, inverses, total, fetched, halves, heard,
    core_send, core_recv, far_send, far_recv, back_send, back_recv,
):
    height = panel.shape[0]
    cut = PT2 * TILE
    me = lax.axis_index("row")
    core = lax.rem(me, 2)
    place = lax.div(me, 2)
    chips = ranks // 2
    partner = place * 2 + 1 - core
    peers = [lax.rem(place + d, chips) * 2 + core for d in range(1, chips)]
    other_half = PT2 * PT2 + PIVOT_TILES
    parts = ((0, PIVOT_TILES // 2, 0), (PIVOT_TILES, other_half // 2, PIVOT_TILES // 2))

    barrier = pltpu.get_barrier_semaphore()
    for device in [partner] + peers:
        pl.semaphore_signal(
            barrier, inc=1, device_id={"row": device}, device_id_type=pl.DeviceIdType.MESH
        )
    pl.semaphore_wait(barrier, chips)

    def copy(source, target, send, recv, device):
        return pltpu.make_async_remote_copy(
            src_ref=source,
            dst_ref=target,
            send_sem=send,
            recv_sem=recv,
            device_id={"row": device},
            device_id_type=pl.DeviceIdType.MESH,
        )

    near, far, back = [], [], []
    for i, (base, n, off) in enumerate(parts):
        near.append(
            copy(
                dense.at[pl.ds(base + (1 - core) * n, n)],
                fetched.at[pl.ds(off, n)],
                core_send.at[i],
                core_recv.at[i],
                partner,
            )
        )
        near[i].start()
    for i, (base, n, off) in enumerate(parts):
        near[i].wait()
        here = pl.ds(off, n)
        halves[here] = dense[pl.ds(base + core * n, n)] + fetched[here]
        far.append(
            [
                copy(halves.at[here], heard.at[d, here], far_send.at[i, d], far_recv.at[i, d], peer)
                for d, peer in enumerate(peers)
            ]
        )
        for one in far[i]:
            one.start()

    def finish(i):
        base, n, off = parts[i]
        mine = pl.ds(base + core * n, n)
        here = pl.ds(off, n)
        for one in far[i]:
            one.wait()
        value = halves[here]
        for d in range(len(peers)):
            value = value + heard[d, here]
        total[mine] = value
        back = copy(total.at[mine], total.at[mine], back_send.at[i], back_recv.at[i], partner)
        back.start()
        back.wait()

    finish(0)
    for a in range(PT2):
        for b in range(a, PT2):
            front[a * TILE : (a + 1) * TILE, b * TILE : (b + 1) * TILE] = total[tile_number(a, b)]
    column[...] = jnp.zeros_like(column)
    r = lax.broadcasted_iota(jnp.int32, (TILE, TILE), 0)
    c = lax.broadcasted_iota(jnp.int32, (TILE, TILE), 1)

    def step(p, _):
        for q in range(PT2):

            @pl.when(p == q)
            def _():
                here = slice(q * TILE, (q + 1) * TILE)
                load_tile(work, twin, 1, 0, front[here, here])

        factor_tiles(work, twin, 1)
        for q in range(PT2):

            @pl.when(p == q)
            def _():
                here = slice(q * TILE, (q + 1) * TILE)
                edge = (q + 1) * TILE
                column[here, here] = jnp.where(r >= c, work[:TILE, :].T, 0.0)
                inverses[q] = work[TILE:, :]
                if q == PT2 - 1:
                    return
                x = dot_nn(work[TILE:, :], front[here, edge:cut])
                xt = x.T
                column[edge:cut, here] = xt
                front[edge:cut, edge:cut] = front[edge:cut, edge:cut] - dot_nn(xt, x)

        return 0

    lax.fori_loop(0, PT2, step, 0)
    finish(1)
    for q in range(PT2):
        here = slice(q * TILE, (q + 1) * TILE)
        right = jnp.concatenate([total[tile_number(q, b)] for b in range(PT2, PT)], axis=1)
        if q:
            right = right - dot_nn(column[here, : q * TILE], front[: q * TILE, cut:])
        front[here, cut:] = dot_nn(inverses[q], right)
    x = front[:cut, cut:]
    xt = x.T
    column[cut:, :] = xt
    for a in range(PT2, PT):
        for b in range(a, PT):
            tile = total[tile_number(a, b)]
            if a == b:
                tile = jnp.where(r <= c, tile, tile.T)
            else:
                front[b * TILE : (b + 1) * TILE, a * TILE : (a + 1) * TILE] = tile.T
            front[a * TILE : (a + 1) * TILE, b * TILE : (b + 1) * TILE] = tile
    front[cut:, cut:] = front[cut:, cut:] - dot_nn(xt, x)
    first = pl.multiple_of(me * height, TILE)
    panel[...] = column[pl.ds(first, height), :]

    @pl.when(first >= cut)
    def _():
        rest[...] = front[pl.ds(first, height), cut:]

    @pl.when(first < cut)
    def _():
        rest[...] = jnp.zeros_like(rest)


def params(**more):
    return pltpu.CompilerParams(vmem_limit_bytes=VMEM_BYTES, **more)


VM = pl.BlockSpec(memory_space=pltpu.VMEM)
SM = pl.BlockSpec(memory_space=pltpu.SMEM)


def run_children(fronts, parents, places, groups):
    kids, order, _ = fronts.shape
    return pl.pallas_call(
        functools.partial(child_kernel, groups),
        in_specs=[pl.BlockSpec(memory_space=pl.ANY), pl.BlockSpec(memory_space=pl.ANY), VM],
        out_specs=[VM, VM, VM],
        out_shape=[
            jax.ShapeDtypeStruct((kids, order - S1, S1), jnp.bfloat16),
            jax.ShapeDtypeStruct((groups // 2 * CAP, SLOT, TILE), F32),
            jax.ShapeDtypeStruct((kids, SLOT, TILE), F32),
        ],
        scratch_shapes=[
            pltpu.VMEM((kids, order, order), F32),
            pltpu.VMEM((2 * kids * TILE, TILE), F32),
            pltpu.VMEM((2 * kids * TILE, TILE), F32),
            pltpu.SMEM(parents.shape, jnp.int32),
            pltpu.SMEM(places.shape, jnp.int32),
            pltpu.SemaphoreType.DMA((2,)),
        ],
        compiler_params=params(),
        name="children",
    )(parents, places, fronts)


def run_exchange(near, far, groups):
    mates = groups // 2 - 1
    dma = pltpu.SemaphoreType.DMA
    return pl.pallas_call(
        functools.partial(exchange_kernel, groups),
        in_specs=[VM, VM],
        out_specs=VM,
        out_shape=jax.ShapeDtypeStruct((groups * CAP, SLOT, TILE), F32),
        scratch_shapes=[
            pltpu.VMEM(far.shape, F32),
            pltpu.VMEM(near.shape, F32),
            dma((CHUNKS,)),
            dma((CHUNKS,)),
            dma((mates,)),
            dma((mates,)),
            dma((CHUNKS, mates)),
            dma((CHUNKS, mates)),
        ],
        compiler_params=params(collective_id=2, has_side_effects=True),
        name="exchange",
    )(near, far)


def run_gather(tiles, slots, parent):
    return pl.pallas_call(
        gather_kernel,
        in_specs=[SM, VM, VM],
        out_specs=VM,
        out_shape=jax.ShapeDtypeStruct((ALL_TILES, TILE, TILE), F32),
        compiler_params=params(),
        name="assemble",
    )(tiles, slots, parent)


def run_parent(dense, height):
    ranks = lax.axis_size("row")
    peers = max(1, ranks // 2 - 1)
    half = ALL_TILES // 2
    dma = pltpu.SemaphoreType.DMA
    return pl.pallas_call(
        functools.partial(parent_kernel, ranks),
        in_specs=[VM],
        out_specs=[VM, VM],
        out_shape=[
            jax.ShapeDtypeStruct((height, PT2 * TILE), F32),
            jax.ShapeDtypeStruct((height, (PT - PT2) * TILE), F32),
        ],
        scratch_shapes=[
            pltpu.VMEM((PT * TILE, PT * TILE), F32),
            pltpu.VMEM((PT * TILE, PT2 * TILE), F32),
            pltpu.VMEM((2 * TILE, TILE), F32),
            pltpu.VMEM((2 * TILE, TILE), F32),
            pltpu.VMEM((PT2, TILE, TILE), F32),
            pltpu.VMEM((ALL_TILES, TILE, TILE), F32),
            pltpu.VMEM((half, TILE, TILE), F32),
            pltpu.VMEM((half, TILE, TILE), F32),
            pltpu.VMEM((peers, half, TILE, TILE), F32),
            dma((2,)),
            dma((2,)),
            dma((2, peers)),
            dma((2, peers)),
            dma((2,)),
            dma((2,)),
        ],
        compiler_params=params(collective_id=1, has_side_effects=True),
        name="parent",
    )(dense)


def local(child_fronts, child_tiles, child_parent, parent_front):
    groups = lax.axis_size("col")
    child_lower, near, far = run_children(child_fronts, child_parent, child_tiles, groups)
    received = run_exchange(near, far, groups)
    received_tiles = received[:, 1, :RT1].astype(jnp.int32)
    dense = run_gather(received_tiles, received, parent_front[0])
    parent_panel, parent_rest = run_parent(dense, parent_front.shape[1])
    return (child_lower, parent_panel[None], parent_rest[None])


def solution(mesh):
    placed = (
        P(("row", "col"), None, None),
        P(("row", "col"), None),
        P(("row", "col"), None),
        P("col", "row", None),
    )
    return jax.shard_map(
        local,
        mesh=mesh,
        in_specs=placed,
        out_specs=(P(("row", "col"), None, None), P("col", "row", None), P("col", "row", None)),
        check_vma=False,
    )
```
